32 devices in a mesh: grp: 2 (over x), row: 16 (over z, y, core).
Axes of the slice: x: 2, y: 2, z: 4, core: 2. Of those that a mesh axis runs over, the one named last changes fastest.
Arguments:
- pair: bfloat16 [64, 32, 128], P(('grp', 'row')), parts along dimension 0, may hold values from -6 to 6
- chain_counts: int32 [8], P('grp'), parts along dimension 0, may hold values from 4 to 8
- w_out_proj: bfloat16 [128, 640], replicated, may hold values from -0.5 to 0.5
- w_out_final: bfloat16 [128, 128], replicated, may hold values from -0.5 to 0.5
- w_in_proj: bfloat16 [128, 640], replicated, may hold values from -0.5 to 0.5
- w_in_final: bfloat16 [128, 128], replicated, may hold values from -0.5 to 0.5
- cotangent: bfloat16 [64, 32, 128], P(('grp', 'row')), parts along dimension 0, may hold values from -6 to 6
Outputs:
- pair_out: bfloat16 [64, 32, 128], P(('grp', 'row')), parts along dimension 0
- pair_grad: bfloat16 [64, 32, 128], P(('grp', 'row')), parts along dimension 0
The draws below stay inside these ranges and needn't reach their ends.
There are 2 independent parts, one for each index of `grp`. The reference program is written for one: setup_inputs(seed, part) draws one part's arguments, and reference() takes and returns one part's arrays. A program takes and returns all parts, laid end to end along the dimension named above; an argument that names none is the same for every part. Nothing has to cross between parts.
Inputs may be any that keep to these rules, and one draw needn't show every extreme that they name: `chain_counts`: tokens of a chain beyond its count, within its 8 slots, are padding.
All inputs are finite; a program needn't handle non-finite values.
Results may differ from the reference program's by a relative error of at most 0.017.
Values may be sent and summed in bfloat16 or wider, within the bound.
A program may use at most 64 MiB of HBM per device.

```python
import jax
import jax.numpy as jnp
from jax import lax

C = 128
CH = 128
CHAINS = 4
N = 32
SLOT = 8


def set_ends(drawn, stream_key, least, high):
    shape = drawn.shape
    spot = [jax.random.randint(jax.random.fold_in(stream_key, axis), (), 0, shape[axis]) for axis in range(len(shape))]
    drawn = drawn.at[tuple(spot)].set(least)
    longest = shape.index(max(shape))
    spot[longest] = (spot[longest] + 1) % shape[longest]
    return drawn.at[tuple(spot)].set(high)


def steps_of(key, shape, split, low, largest):
    def one(axis_at, parts):
        heights = jax.random.uniform(jax.random.fold_in(jax.random.fold_in(key, 6), axis_at), (parts,), jnp.float32, low / len(split), largest / len(split))
        return jnp.repeat(jnp.exp(heights), shape[axis_at] // parts).reshape((-1,) + (1,) * (len(shape) - axis_at - 1))

    factor_of = one(*split[0])
    for cut in split[1:]:
        factor_of = factor_of * one(*cut)
    return factor_of


def normal_values(stream_key, extent, scale, reach, pieces=(), kind=jnp.bfloat16):
    result = scale * jax.random.normal(stream_key, extent, jnp.float32)
    if pieces:
        result = result * steps_of(stream_key, extent, pieces, -0.22, 0.18)
    return jnp.clip(result, -reach, reach).astype(kind)


def setup_inputs(seed: int = 0, part: int = 0) -> dict:
    arg_keys = jax.random.split(jax.random.key(seed), 8)
    part_splits = jax.random.split(jax.random.fold_in(arg_keys[7], part), 8)
    return {
        "pair": normal_values(part_splits[0], (N, N, C), 1.0, 6.0, ((0, 16),)),
        "chain_counts": set_ends(jax.random.randint(part_splits[1], (CHAINS,), SLOT // 2, SLOT + 1), jax.random.fold_in(part_splits[1], 1), SLOT // 2, SLOT).astype(jnp.int32),
        "w_out_proj": normal_values(arg_keys[2], (C, 4 * CH + C), C ** -0.5, 0.5),
        "w_out_final": normal_values(arg_keys[3], (CH, C), CH ** -0.5, 0.5),
        "w_in_proj": normal_values(arg_keys[4], (C, 4 * CH + C), C ** -0.5, 0.5),
        "w_in_final": normal_values(arg_keys[5], (CH, C), CH ** -0.5, 0.5),
        "cotangent": normal_values(part_splits[6], (N, N, C), 1.0, 6.0, ((0, 16),)),
    }


def token_valid(positions, counts, slot):
    chain = positions // slot
    labels = jnp.arange(counts.shape[0], dtype=jnp.int32)
    own = lax.optimization_barrier(jnp.sum(jnp.where(chain[:, None] == labels[None, :], counts[None, :], 0), axis=1))
    return (positions % slot < own).astype(jnp.float32)

def normalize(values):
    center = values - lax.optimization_barrier(jnp.mean(values, axis=-1, keepdims=True))
    spread = lax.optimization_barrier(jnp.mean(center * center, axis=-1, keepdims=True))
    return center * jax.lax.rsqrt(spread + 1e-05)

def project(zfloat, mask, weight):
    hidden = weight.shape[1] // 4 - weight.shape[0] // 4
    width = zfloat.shape[-1]
    normed = normalize(zfloat).astype(jnp.bfloat16)
    lead = normed.shape[:-1]
    mixed = jnp.dot(normed.reshape(-1, width), weight, preferred_element_type=jnp.float32)
    mixed = mixed.reshape(lead + (weight.shape[1],))
    a_proj = mixed[..., :hidden]
    a_gate = mixed[..., hidden:2 * hidden]
    b_proj = mixed[..., 2 * hidden:3 * hidden]
    b_gate = mixed[..., 3 * hidden:4 * hidden]
    out_gate = jax.nn.sigmoid(mixed[..., 4 * hidden:])
    left = (mask[..., None] * jax.nn.sigmoid(a_gate) * a_proj).astype(jnp.bfloat16)
    right = (mask[..., None] * jax.nn.sigmoid(b_gate) * b_proj).astype(jnp.bfloat16)
    return (left, right, out_gate)

def finish(contracted, out_gate, zfloat, final):
    normed = normalize(contracted).astype(jnp.bfloat16)
    lead = normed.shape[:-1]
    update = jnp.dot(normed.reshape(-1, final.shape[0]), final, preferred_element_type=jnp.float32)
    return zfloat + out_gate * update.reshape(lead + (final.shape[1],))

def float_einsum(form, first, second):
    return jnp.einsum(form, first.astype(jnp.float32), second.astype(jnp.float32))

def reference(pair, chain_counts, w_out_proj, w_out_final, w_in_proj, w_in_final, cotangent):
    positions = jnp.arange(N, dtype=jnp.int32)
    valid = token_valid(positions, chain_counts, SLOT)
    mask = valid[:, None] * valid[None, :]
    start_float = pair.astype(jnp.float32)
    left1, right1, gate1 = project(start_float, mask, w_out_proj)
    inner1 = float_einsum('ikc,jkc->ijc', left1, right1)
    middle = finish(inner1, gate1, start_float, w_out_final).astype(jnp.bfloat16)
    middle_float = middle.astype(jnp.float32)
    left2, right2, gate2 = project(middle_float, mask, w_in_proj)
    inner2 = float_einsum('kic,kjc->ijc', left2, right2)
    pair_out = finish(inner2, gate2, middle_float, w_in_final).astype(jnp.bfloat16)
    _, finish_back2 = jax.vjp(lambda x, g, z: finish(x, g, z, w_in_final), inner2, gate2, middle_float)
    d_inner2, d_gate2, d_direct1 = finish_back2(cotangent.astype(jnp.float32))
    d_inner2 = d_inner2.astype(jnp.bfloat16)
    d_left2 = float_einsum('ijc,kjc->kic', d_inner2, right2).astype(jnp.bfloat16)
    d_right2 = float_einsum('ijc,kic->kjc', d_inner2, left2).astype(jnp.bfloat16)
    _, project_back2 = jax.vjp(lambda z: project(z, mask, w_in_proj), middle_float)
    d_proj1, = project_back2((d_left2, d_right2, d_gate2))
    grad_middle = d_direct1 + d_proj1
    _, finish_back1 = jax.vjp(lambda x, g, z: finish(x, g, z, w_out_final), inner1, gate1, start_float)
    d_inner1, d_gate1, d_direct0 = finish_back1(grad_middle)
    d_inner1 = d_inner1.astype(jnp.bfloat16)
    d_left1 = float_einsum('ijc,jkc->ikc', d_inner1, right1).astype(jnp.bfloat16)
    d_right1 = float_einsum('ijc,ikc->jkc', d_inner1, left1).astype(jnp.bfloat16)
    _, project_back1 = jax.vjp(lambda z: project(z, mask, w_out_proj), start_float)
    d_proj0, = project_back1((d_left1, d_right1, d_gate1))
    pair_grad = (d_direct0 + d_proj0).astype(jnp.bfloat16)
    return (pair_out, pair_grad)
```

```python
import functools

import jax
import jax.numpy as jnp
from jax import lax
from jax.experimental import pallas as pl
from jax.experimental.pallas import tpu as pltpu
from jax.sharding import PartitionSpec as P


def token_valid(positions, counts, slot):
    chain = positions // slot
    labels = jnp.arange(counts.shape[0], dtype=jnp.int32)
    own = jnp.sum(jnp.where(chain[:, None] == labels[None, :], counts[None, :], 0), axis=1)
    return (positions % slot < own).astype(jnp.float32)


def normalize(values):
    center = values - jnp.mean(values, axis=-1, keepdims=True)
    spread = jnp.mean(center * center, axis=-1, keepdims=True)
    return center * jax.lax.rsqrt(spread + 1e-05)


def project(zfloat, mask, weight):
    hidden = weight.shape[1] // 4 - weight.shape[0] // 4
    width = zfloat.shape[-1]
    normed = normalize(zfloat).astype(jnp.bfloat16)
    lead = normed.shape[:-1]
    mixed = jnp.dot(normed.reshape(-1, width), weight, preferred_element_type=jnp.float32)
    mixed = mixed.reshape(lead + (weight.shape[1],))
    a_proj = mixed[..., :hidden]
    a_gate = mixed[..., hidden : 2 * hidden]
    b_proj = mixed[..., 2 * hidden : 3 * hidden]
    b_gate = mixed[..., 3 * hidden : 4 * hidden]
    out_gate = jax.nn.sigmoid(mixed[..., 4 * hidden :])
    left = (mask[..., None] * jax.nn.sigmoid(a_gate) * a_proj).astype(jnp.bfloat16)
    right = (mask[..., None] * jax.nn.sigmoid(b_gate) * b_proj).astype(jnp.bfloat16)
    return (left, right, out_gate)


def finish(contracted, out_gate, zfloat, final):
    normed = normalize(contracted).astype(jnp.bfloat16)
    lead = normed.shape[:-1]
    update = jnp.dot(normed.reshape(-1, final.shape[0]), final, preferred_element_type=jnp.float32)
    return zfloat + out_gate * update.reshape(lead + (final.shape[1],))


def contract(form, first, second):
    return jnp.einsum(form, first, second, preferred_element_type=jnp.float32)


def body(pair, chain_counts, w_out_proj, w_out_final, w_in_proj, w_in_final, cotangent):
    rows = pair.shape[0]
    tokens = pair.shape[1]
    slot = tokens // chain_counts.shape[0]
    positions = jnp.arange(tokens, dtype=jnp.int32)
    own_rows = lax.axis_index("row") * rows + jnp.arange(rows, dtype=jnp.int32)
    mask = (
        token_valid(own_rows, chain_counts, slot)[:, None]
        * token_valid(positions, chain_counts, slot)[None, :]
    )
    start_float = pair.astype(jnp.float32)
    left1, right1, gate1 = project(start_float, mask, w_out_proj)
    inner1 = contract("ikc,jkc->ijc", left1, lax.all_gather(right1, "row", axis=0, tiled=True))
    middle = finish(inner1, gate1, start_float, w_out_final).astype(jnp.bfloat16)
    middle_float = middle.astype(jnp.float32)
    left2, right2, gate2 = project(middle_float, mask, w_in_proj)
    left_turned, right_turned = (
        lax.all_to_all(left2, "row", split_axis=1, concat_axis=0, tiled=True),
        lax.all_to_all(right2, "row", split_axis=1, concat_axis=0, tiled=True),
    )
    inner2 = contract(
        "kic,kjc->ijc", left_turned, lax.all_gather(right_turned, "row", axis=1, tiled=True)
    )
    pair_out = finish(inner2, gate2, middle_float, w_in_final).astype(jnp.bfloat16)
    _, finish_back2 = jax.vjp(
        lambda x, g, z: finish(x, g, z, w_in_final), inner2, gate2, middle_float
    )
    d_inner2, d_gate2, d_direct1 = finish_back2(cotangent.astype(jnp.float32))
    d_inner2 = d_inner2.astype(jnp.bfloat16)
    piece = lax.all_gather(d_inner2, "row", axis=0, tiled=True)
    block = contract("kjc,ijc->kic", right2, piece)
    d_right = contract("kic,ijc->kjc", left2, piece)
    _, project_back2 = jax.vjp(lambda z: project(z, mask, w_in_proj), middle_float)
    (d_proj1,) = project_back2((block.astype(jnp.bfloat16), d_right.astype(jnp.bfloat16), d_gate2))
    grad_middle = d_direct1 + d_proj1
    _, finish_back1 = jax.vjp(
        lambda x, g, z: finish(x, g, z, w_out_final), inner1, gate1, start_float
    )
    d_inner1, d_gate1, d_direct0 = finish_back1(grad_middle)
    d_inner1 = d_inner1.astype(jnp.bfloat16)
    d_left1 = contract("ijc,jkc->ikc", d_inner1, lax.all_gather(right1, "row", axis=0, tiled=True))
    d_turned = lax.all_to_all(d_inner1, "row", split_axis=1, concat_axis=0, tiled=True)
    d_right1 = contract("ijc,ikc->jkc", d_turned, lax.all_gather(left1, "row", axis=0, tiled=True))
    _, project_back1 = jax.vjp(lambda z: project(z, mask, w_out_proj), start_float)
    (d_proj0,) = project_back1(
        (d_left1.astype(jnp.bfloat16), d_right1.astype(jnp.bfloat16), d_gate1)
    )
    pair_grad = (d_direct0 + d_proj0).astype(jnp.bfloat16)
    return (pair_out, pair_grad)


F32 = jnp.float32
BF16 = jnp.bfloat16
EPS = 1e-05


def sigmoid(x):
    return 0.5 * jnp.tanh(0.5 * x) + 0.5


def matmul(x, w):
    return jnp.dot(x.astype(BF16), w, preferred_element_type=F32)


def matmul_t(x, w):
    return lax.dot_general(x.astype(BF16), w, (((1,), (1,)), ((), ())), preferred_element_type=F32)


def mean(x):
    return jnp.mean(x, axis=-1, keepdims=True)


def layer_norm(x):
    center = x - mean(x)
    scale = lax.rsqrt(mean(center * center) + EPS)
    return center * scale, scale


def layer_norm_back(grad, hat, scale):
    return scale * (grad - mean(grad) - hat * mean(grad * hat))


def rounded(x):
    return x.astype(BF16).astype(F32)


def gates(hidden, c):
    part = [hidden[:, i * c : (i + 1) * c] for i in range(5)]
    return part[0], sigmoid(part[1]), part[2], sigmoid(part[3]), sigmoid(part[4])


def project_back(da, db, dgate, mask, saved, hat, scale, weight):
    ap, sa, bp, sb, gate = saved
    ma, mb = mask * da * sa, mask * db * sb
    parts = [ma, ma * ap * (1.0 - sa), mb, mb * bp * (1.0 - sb), dgate * gate * (1.0 - gate)]
    dhidden = jnp.concatenate([p.astype(BF16) for p in parts], axis=1)
    return layer_norm_back(rounded(matmul_t(dhidden, weight)), hat, scale)


def kernel(
    n, rows, tokens, chunk, slot,
    pair_in, counts, w1_in, v1_in, w2_in, v2_in, cot_in,
    out_ref, grad_ref,
    pair_all, cot_all, w1, v1, w2, v2,
    mask, a1, b1, gate1, x, mid, a2, b2, gate2, dx, saved1, send_buf, recv_buf,
    local_sem, own_sem, pair_send, pair_recv, cot_send, cot_recv, turn_send, turn_recv,
):
    me = lax.axis_index("row")
    core = lax.rem(me, 2)
    chip = me // 2
    chips = n // 2
    sibling = me + 1 - 2 * core
    own = rows * tokens
    c = out_ref.shape[1]
    slotrows = 8

    def device(i):
        return {"row": i}

    loads = [
        pltpu.make_async_copy(s, d, local_sem.at[i])
        for i, (s, d) in enumerate([(w1_in, w1), (v1_in, v1), (w2_in, w2), (v2_in, v2)])
    ]
    own_block = pl.ds(pl.multiple_of(me * own, own), own)
    own_loads = [
        pltpu.make_async_copy(pair_in, pair_all.at[own_block], own_sem.at[0]),
        pltpu.make_async_copy(cot_in, cot_all.at[own_block], own_sem.at[1]),
    ]
    for copy in own_loads + loads:
        copy.start()

    barrier = pltpu.get_barrier_semaphore()
    for t in range(1, n):
        pl.semaphore_signal(
            barrier, inc=1, device_id=device(lax.rem(me + t, n)),
            device_id_type=pl.DeviceIdType.MESH,
        )

    def valid(index):
        chain = index // slot
        count = jnp.zeros(index.shape, jnp.int32)
        for i in range(counts.shape[0]):
            count = jnp.where(chain == i, counts[i], count)
        return jnp.where(index - chain * slot < count, 1.0, 0.0)

    second = valid(lax.broadcasted_iota(jnp.int32, (tokens, c), 0))
    for i in range(tokens):
        first = valid(jnp.full((tokens, c), i, jnp.int32))
        mask[i * tokens : (i + 1) * tokens, :] = first * second

    pl.semaphore_wait(barrier, n - 1)

    def gather_sends(source, whole, send_sem, recv_sem):
        copies = []
        for t in range(chips):
            target = sibling if t == 0 else lax.rem(chip + t, chips) * 2 + core
            copies.append(
                pltpu.make_async_remote_copy(
                    src_ref=source, dst_ref=whole.at[own_block],
                    send_sem=send_sem.at[t], recv_sem=recv_sem.at[me],
                    device_id=device(target), device_id_type=pl.DeviceIdType.MESH,
                )
            )
        return copies

    def block_copy(whole, send_sem, recv_sem, index, send_index):
        block = whole.at[pl.ds(pl.multiple_of(index * own, own), own)]
        return pltpu.make_async_remote_copy(
            src_ref=block, dst_ref=block,
            send_sem=send_sem.at[send_index], recv_sem=recv_sem.at[index],
            device_id=device(sibling), device_id_type=pl.DeviceIdType.MESH,
        )

    def forward(whole, send_sem, recv_sem):
        copies = []
        for t in range(1, chips):
            source = lax.rem(chip + chips - t, chips) * 2 + core
            copy = block_copy(whole, send_sem, recv_sem, source, chips - 1 + t)
            copy.wait_recv()
            copy.start()
            copies.append(copy)
        return copies

    def wait_forwarded(whole, send_sem, recv_sem):
        for t in range(chips):
            source = lax.rem(chip + chips - t, chips) * 2 + 1 - core
            block_copy(whole, send_sem, recv_sem, source, 0).wait_recv()

    pair_copies = gather_sends(pair_in, pair_all, pair_send, pair_recv)
    for copy in pair_copies:
        copy.start()
    for copy in own_loads + loads:
        copy.wait()

    z_own = pair_all[own_block, :].astype(F32)
    hat, scale = layer_norm(z_own)
    for i, part in enumerate(gates(matmul(hat, w1[...]), c)):
        saved1[i] = part

    pair_copies += forward(pair_all, pair_send, pair_recv)
    cot_copies = gather_sends(cot_in, cot_all, cot_send, cot_recv)
    for copy in cot_copies:
        copy.start()
    wait_forwarded(pair_all, pair_send, pair_recv)

    whole_rows = tokens * tokens

    def chunks(body):
        def step(i, carry):
            body(pl.ds(pl.multiple_of(i * chunk, chunk), chunk))
            return carry

        lax.fori_loop(0, whole_rows // chunk, step, 0)

    def project1(at):
        hat, _ = layer_norm(pair_all[at, :].astype(F32))
        ap, sa, bp, sb, gate = gates(matmul(hat, w1[...]), c)
        m = mask[at, :]
        a1[at, :] = rounded(m * sa * ap)
        b1[at, :] = rounded(m * sb * bp)
        gate1[at, :] = gate

    chunks(project1)
    wide = 4

    def product1(ib, carry):
        base = ib * (wide * tokens)
        sums = [jnp.zeros((tokens, c), F32) for _ in range(wide)]
        for k in range(tokens):
            block = b1[pl.ds(k, tokens, stride=tokens), :]
            for u in range(wide):
                sums[u] = sums[u] + a1[pl.ds(base + (u * tokens + k), 1), :] * block
        for u in range(wide):
            x[pl.ds(pl.multiple_of(base + u * tokens, tokens), tokens), :] = sums[u]
        return carry

    lax.fori_loop(0, tokens // wide, product1, 0)

    cot_copies += forward(cot_all, cot_send, cot_recv)

    def finish1(at):
        y, _ = layer_norm(x[at, :])
        middle = rounded(pair_all[at, :].astype(F32) + gate1[at, :] * matmul(y, v1[...]))
        mid[at, :] = middle
        hat, _ = layer_norm(middle)
        ap, sa, bp, sb, gate = gates(matmul(hat, w2[...]), c)
        m = mask[at, :]
        a2[at, :] = rounded(m * sa * ap)
        b2[at, :] = rounded(m * sb * bp)
        gate2[at, :] = gate

    chunks(finish1)
    x1_hat, x1_scale = layer_norm(x[own_block, :])
    update1 = matmul(x1_hat, v1[...])

    def product2(ib, carry):
        base = ib * wide
        sums = [jnp.zeros((tokens, c), F32) for _ in range(wide)]
        for k in range(tokens):
            block = b2[k * tokens : (k + 1) * tokens, :]
            for u in range(wide):
                sums[u] = sums[u] + a2[pl.ds(base + (k * tokens + u), 1), :] * block
        for u in range(wide):
            x[pl.ds(pl.multiple_of((base + u) * tokens, tokens), tokens), :] = sums[u]
        return carry

    lax.fori_loop(0, tokens // wide, product2, 0)

    wait_forwarded(cot_all, cot_send, cot_recv)

    def back2(at):
        hat, scale = layer_norm(x[at, :])
        dy = rounded(matmul_t(cot_all[at, :].astype(F32) * gate2[at, :], v2[...]))
        dx[at, :] = rounded(layer_norm_back(dy, hat, scale))

    chunks(back2)

    def own_rows(left, left_stride, right):
        sums = [jnp.zeros((tokens, c), F32) for _ in range(rows)]
        for t in range(tokens):
            block = right(t)
            for r in range(rows):
                sums[r] = sums[r] + left(r, t) * block
        return rounded(jnp.concatenate(sums, axis=0))

    m_own = mask[own_block, :]
    cot_own = cot_all[own_block, :].astype(F32)
    mid_own = mid[own_block, :]
    y2, _ = layer_norm(x[own_block, :])
    update2 = matmul(y2, v2[...])
    gate2_own = gate2[own_block, :]
    out_ref[...] = (mid_own + gate2_own * update2).astype(BF16)
    start = me * own
    da2 = own_rows(
        lambda r, t: b2[pl.ds(start + (r * tokens + t), 1), :], 0,
        lambda t: dx[pl.ds(t, tokens, stride=tokens), :],
    )
    db2 = own_rows(
        lambda r, t: a2[pl.ds(start + (r * tokens + t), 1), :], 0,
        lambda t: dx[t * tokens : (t + 1) * tokens, :],
    )
    hat2, scale2 = layer_norm(mid_own)
    saved2 = gates(matmul(hat2, w2[...]), c)
    grad1 = cot_own + project_back(
        da2, db2, cot_own * update2, m_own, saved2, hat2, scale2, w2[...]
    )

    dy1 = rounded(matmul_t(grad1 * saved1[4], v1[...]))
    dx1 = rounded(layer_norm_back(dy1, x1_hat, x1_scale))
    x[0:own, :] = dx1
    for r in range(rows):
        for s in range(rows):
            send_buf[pl.ds(r * rows + s, n, stride=slotrows), :] = x[
                pl.ds(r * tokens + s, n, stride=rows), :
            ]

    def turn_block(ref, i):
        return ref.at[pl.ds(pl.multiple_of(i * slotrows, slotrows), slotrows)]

    turns = []
    for t in range(1, n):
        target = lax.rem(me + t, n)
        turns.append(
            pltpu.make_async_remote_copy(
                src_ref=turn_block(send_buf, target), dst_ref=turn_block(recv_buf, me),
                send_sem=turn_send.at[t], recv_sem=turn_recv.at[t],
                device_id=device(target), device_id_type=pl.DeviceIdType.MESH,
            )
        )
    for copy in turns:
        copy.start()
    mine = pl.ds(pl.multiple_of(me * slotrows, slotrows), slotrows)
    recv_buf[mine, :] = send_buf[mine, :]

    da1 = own_rows(
        lambda r, t: x[r * tokens + t : r * tokens + t + 1, :], 0,
        lambda t: b1[t * tokens : (t + 1) * tokens, :],
    )
    for t in range(1, n):
        source = lax.rem(me + n - t, n)
        pltpu.make_async_remote_copy(
            src_ref=turn_block(send_buf, me), dst_ref=turn_block(recv_buf, source),
            send_sem=turn_send.at[t], recv_sem=turn_recv.at[t],
            device_id=device(source), device_id_type=pl.DeviceIdType.MESH,
        ).wait_recv()

    def turned(r, t):
        at = (t // rows) * slotrows + (t % rows) * rows + r
        return recv_buf[at : at + 1, :]

    db1 = own_rows(turned, 0, lambda t: a1[t * tokens : (t + 1) * tokens, :])
    saved = [saved1[i] for i in range(5)]
    hat1, scale1 = layer_norm(pair_all[own_block, :].astype(F32))
    grad0 = grad1 + project_back(
        da1, db1, grad1 * update1, m_own, saved, hat1, scale1, w1[...]
    )
    grad_ref[...] = grad0.astype(BF16)
    for copy in pair_copies + cot_copies + turns:
        copy.wait_send()


def fused(n, pair, chain_counts, w1, v1, w2, v2, cotangent):
    rows, tokens, c = pair.shape
    own, whole = rows * tokens, tokens * tokens
    any_spec = pl.BlockSpec(memory_space=pl.ANY)
    vmem_spec = pl.BlockSpec(memory_space=pltpu.VMEM)
    result = jax.ShapeDtypeStruct((own, c), BF16)
    full = pltpu.VMEM((whole, c), F32)
    chunk = min(whole, 256)
    turn = pltpu.VMEM((n * 8, c), F32)
    out, grad = pl.pallas_call(
        functools.partial(kernel, n, rows, tokens, chunk, tokens // chain_counts.shape[0]),
        out_shape=(result, result),
        in_specs=[any_spec, pl.BlockSpec(memory_space=pltpu.SMEM)] + [any_spec] * 5,
        out_specs=(vmem_spec, vmem_spec),
        scratch_shapes=[pltpu.VMEM((whole, c), BF16)] * 2
        + [pltpu.VMEM(w.shape, BF16) for w in (w1, v1, w2, v2)]
        + [full] * 10
        + [pltpu.VMEM((5, own, c), F32), turn, turn]
        + [
            pltpu.SemaphoreType.DMA((4,)),
            pltpu.SemaphoreType.DMA((2,)),
            pltpu.SemaphoreType.DMA((n,)),
            pltpu.SemaphoreType.DMA((n,)),
            pltpu.SemaphoreType.DMA((n,)),
            pltpu.SemaphoreType.DMA((n,)),
            pltpu.SemaphoreType.DMA((n,)),
            pltpu.SemaphoreType.DMA((n,)),
        ],
        compiler_params=pltpu.CompilerParams(
            collective_id=0, has_side_effects=True, vmem_limit_bytes=48 * 2**20
        ),
    )(pair.reshape(own, c), chain_counts, w1, v1, w2, v2, cotangent.reshape(own, c))
    return out.reshape(pair.shape), grad.reshape(pair.shape)


def solution(mesh):
    in_specs = (
        P(("grp", "row"), None, None),
        P("grp"),
        P(),
        P(),
        P(),
        P(),
        P(("grp", "row"), None, None),
    )
    out_specs = (P(("grp", "row"), None, None), P(("grp", "row"), None, None))
    n = mesh.shape["row"]

    def run(pair, chain_counts, w1, v1, w2, v2, cotangent):
        rows, tokens, c = pair.shape
        small = tokens <= 32 and rows * rows <= 8 and tokens % 8 == 0 and n % 2 == 0
        if small and (rows * tokens) % 16 == 0 and w1.shape[1] == 5 * c and c == 128:
            return fused(n, pair, chain_counts, w1, v1, w2, v2, cotangent)
        return body(pair, chain_counts, w1, v1, w2, v2, cotangent)

    return jax.shard_map(run, mesh=mesh, in_specs=in_specs, out_specs=out_specs, check_vma=False)
```

```python
import functools

import jax
import jax.numpy as jnp
from jax import lax
from jax.experimental import pallas as pl
from jax.experimental.pallas import tpu as pltpu
from jax.sharding import PartitionSpec as P


def token_valid(positions, counts, slot):
    chain = positions // slot
    labels = jnp.arange(counts.shape[0], dtype=jnp.int32)
    own = jnp.sum(jnp.where(chain[:, None] == labels[None, :], counts[None, :], 0), axis=1)
    return (positions % slot < own).astype(jnp.float32)


def normalize(values):
    center = values - jnp.mean(values, axis=-1, keepdims=True)
    spread = jnp.mean(center * center, axis=-1, keepdims=True)
    return center * jax.lax.rsqrt(spread + 1e-05)


def project(zfloat, mask, weight):
    hidden = weight.shape[1] // 4 - weight.shape[0] // 4
    width = zfloat.shape[-1]
    normed = normalize(zfloat).astype(jnp.bfloat16)
    lead = normed.shape[:-1]
    mixed = jnp.dot(normed.reshape(-1, width), weight, preferred_element_type=jnp.float32)
    mixed = mixed.reshape(lead + (weight.shape[1],))
    a_proj = mixed[..., :hidden]
    a_gate = mixed[..., hidden : 2 * hidden]
    b_proj = mixed[..., 2 * hidden : 3 * hidden]
    b_gate = mixed[..., 3 * hidden : 4 * hidden]
    out_gate = jax.nn.sigmoid(mixed[..., 4 * hidden :])
    left = (mask[..., None] * jax.nn.sigmoid(a_gate) * a_proj).astype(jnp.bfloat16)
    right = (mask[..., None] * jax.nn.sigmoid(b_gate) * b_proj).astype(jnp.bfloat16)
    return (left, right, out_gate)


def finish(contracted, out_gate, zfloat, final):
    normed = normalize(contracted).astype(jnp.bfloat16)
    lead = normed.shape[:-1]
    update = jnp.dot(normed.reshape(-1, final.shape[0]), final, preferred_element_type=jnp.float32)
    return zfloat + out_gate * update.reshape(lead + (final.shape[1],))


def contract(form, first, second):
    return jnp.einsum(form, first, second, preferred_element_type=jnp.float32)


def body(pair, chain_counts, w_out_proj, w_out_final, w_in_proj, w_in_final, cotangent):
    rows = pair.shape[0]
    tokens = pair.shape[1]
    slot = tokens // chain_counts.shape[0]
    positions = jnp.arange(tokens, dtype=jnp.int32)
    own_rows = lax.axis_index("row") * rows + jnp.arange(rows, dtype=jnp.int32)
    mask = (
        token_valid(own_rows, chain_counts, slot)[:, None]
        * token_valid(positions, chain_counts, slot)[None, :]
    )
    start_float = pair.astype(jnp.float32)
    left1, right1, gate1 = project(start_float, mask, w_out_proj)
    inner1 = contract("ikc,jkc->ijc", left1, lax.all_gather(right1, "row", axis=0, tiled=True))
    middle = finish(inner1, gate1, start_float, w_out_final).astype(jnp.bfloat16)
    middle_float = middle.astype(jnp.float32)
    left2, right2, gate2 = project(middle_float, mask, w_in_proj)
    left_turned, right_turned = (
        lax.all_to_all(left2, "row", split_axis=1, concat_axis=0, tiled=True),
        lax.all_to_all(right2, "row", split_axis=1, concat_axis=0, tiled=True),
    )
    inner2 = contract(
        "kic,kjc->ijc", left_turned, lax.all_gather(right_turned, "row", axis=1, tiled=True)
    )
    pair_out = finish(inner2, gate2, middle_float, w_in_final).astype(jnp.bfloat16)
    _, finish_back2 = jax.vjp(
        lambda x, g, z: finish(x, g, z, w_in_final), inner2, gate2, middle_float
    )
    d_inner2, d_gate2, d_direct1 = finish_back2(cotangent.astype(jnp.float32))
    d_inner2 = d_inner2.astype(jnp.bfloat16)
    piece = lax.all_gather(d_inner2, "row", axis=0, tiled=True)
    block = contract("kjc,ijc->kic", right2, piece)
    d_right = contract("kic,ijc->kjc", left2, piece)
    _, project_back2 = jax.vjp(lambda z: project(z, mask, w_in_proj), middle_float)
    (d_proj1,) = project_back2((block.astype(jnp.bfloat16), d_right.astype(jnp.bfloat16), d_gate2))
    grad_middle = d_direct1 + d_proj1
    _, finish_back1 = jax.vjp(
        lambda x, g, z: finish(x, g, z, w_out_final), inner1, gate1, start_float
    )
    d_inner1, d_gate1, d_direct0 = finish_back1(grad_middle)
    d_inner1 = d_inner1.astype(jnp.bfloat16)
    d_left1 = contract("ijc,jkc->ikc", d_inner1, lax.all_gather(right1, "row", axis=0, tiled=True))
    d_turned = lax.all_to_all(d_inner1, "row", split_axis=1, concat_axis=0, tiled=True)
    d_right1 = contract("ijc,ikc->jkc", d_turned, lax.all_gather(left1, "row", axis=0, tiled=True))
    _, project_back1 = jax.vjp(lambda z: project(z, mask, w_out_proj), start_float)
    (d_proj0,) = project_back1(
        (d_left1.astype(jnp.bfloat16), d_right1.astype(jnp.bfloat16), d_gate1)
    )
    pair_grad = (d_direct0 + d_proj0).astype(jnp.bfloat16)
    return (pair_out, pair_grad)


F32 = jnp.float32
BF16 = jnp.bfloat16
EPS = 1e-05


def sigmoid(x):
    return 0.5 * jnp.tanh(0.5 * x) + 0.5


def matmul(x, w):
    return jnp.dot(x.astype(BF16), w, preferred_element_type=F32)


def matmul_t(x, w):
    return lax.dot_general(x.astype(BF16), w, (((1,), (1,)), ((), ())), preferred_element_type=F32)


def mean(x):
    return jnp.mean(x, axis=-1, keepdims=True)


def mean_by_matmul(x):
    c = x.shape[1]
    return jnp.dot(x.astype(BF16), jnp.full((c, c), 1.0 / c, BF16), preferred_element_type=F32)


def layer_norm(x):
    center = x - mean(x)
    scale = lax.rsqrt(mean_by_matmul(center * center) + EPS)
    return center * scale, scale


def layer_norm_back(grad, hat, scale):
    return scale * (grad - mean(grad) - hat * mean(grad * hat))


def rounded(x):
    return x.astype(BF16).astype(F32)


def gates(hidden, c):
    part = [hidden[:, i * c : (i + 1) * c] for i in range(5)]
    return part[0], sigmoid(part[1]), part[2], sigmoid(part[3]), sigmoid(part[4])


def project_back(da, db, dgate, mask, saved, hat, scale, weight):
    ap, sa, bp, sb, gate = saved
    ma, mb = mask * da * sa, mask * db * sb
    parts = [ma, ma * ap * (1.0 - sa), mb, mb * bp * (1.0 - sb), dgate * gate * (1.0 - gate)]
    dhidden = jnp.concatenate([p.astype(BF16) for p in parts], axis=1)
    return layer_norm_back(rounded(matmul_t(dhidden, weight)), hat, scale)


def kernel(
    n, rows, tokens, chunk, slot,
    pair_in, counts_in, w1_in, v1_in, w2_in, v2_in, cot_in,
    both_ref,
    pair_all, cot_all, w1, v1, w2, v2,
    counts, mask, a1, b1, gate1, x, mid, a2, b2, gate2, dx, saved1, send_buf, recv_buf,
    counts_sem, local_sem, own_sem, pair_send, pair_recv, cot_send, cot_recv, turn_send, turn_recv,
):
    me = lax.axis_index("row")
    core = lax.rem(me, 2)
    chip = me // 2
    chips = n // 2
    sibling = me + 1 - 2 * core
    own = rows * tokens
    c = both_ref.shape[1]
    out_ref = both_ref.at[0:own]
    grad_ref = both_ref.at[own : 2 * own]
    slotrows = 8

    def device(i):
        return {"row": i}

    loads = [
        pltpu.make_async_copy(s, d, local_sem.at[i])
        for i, (s, d) in enumerate([(w1_in, w1), (v1_in, v1), (w2_in, w2), (v2_in, v2)])
    ]
    own_block = pl.ds(pl.multiple_of(me * own, own), own)
    own_loads = [
        pltpu.make_async_copy(pair_in, pair_all.at[own_block], own_sem.at[0]),
        pltpu.make_async_copy(cot_in, cot_all.at[own_block], own_sem.at[1]),
    ]
    count_load = pltpu.make_async_copy(counts_in, counts, counts_sem)
    for copy in [count_load] + own_loads + loads:
        copy.start()

    barrier = pltpu.get_barrier_semaphore()
    for t in range(1, n):
        pl.semaphore_signal(
            barrier, inc=1, device_id=device(lax.rem(me + t, n)),
            device_id_type=pl.DeviceIdType.MESH,
        )

    def valid(index):
        chain = index // slot
        count = jnp.zeros(index.shape, jnp.int32)
        for i in range(counts.shape[0]):
            count = jnp.where(chain == i, counts[i], count)
        return jnp.where(index - chain * slot < count, 1.0, 0.0)

    count_load.wait()
    second = valid(lax.broadcasted_iota(jnp.int32, (tokens, c), 0))
    for i in range(tokens):
        first = valid(jnp.full((tokens, c), i, jnp.int32))
        mask[i * tokens : (i + 1) * tokens, :] = first * second

    pl.semaphore_wait(barrier, n - 1)

    def gather_sends(source, whole, send_sem, recv_sem):
        copies = []
        for t in range(chips):
            target = sibling if t == 0 else lax.rem(chip + t, chips) * 2 + core
            copies.append(
                pltpu.make_async_remote_copy(
                    src_ref=source, dst_ref=whole.at[own_block],
                    send_sem=send_sem.at[t], recv_sem=recv_sem.at[me],
                    device_id=device(target), device_id_type=pl.DeviceIdType.MESH,
                )
            )
        return copies

    def block_copy(whole, send_sem, recv_sem, index, send_index):
        block = whole.at[pl.ds(pl.multiple_of(index * own, own), own)]
        return pltpu.make_async_remote_copy(
            src_ref=block, dst_ref=block,
            send_sem=send_sem.at[send_index], recv_sem=recv_sem.at[index],
            device_id=device(sibling), device_id_type=pl.DeviceIdType.MESH,
        )

    def forward(whole, send_sem, recv_sem):
        copies = []
        for t in range(1, chips):
            source = lax.rem(chip + chips - t, chips) * 2 + core
            copy = block_copy(whole, send_sem, recv_sem, source, chips - 1 + t)
            copy.wait_recv()
            copy.start()
            copies.append(copy)
        return copies

    def wait_forwarded(whole, send_sem, recv_sem):
        for t in range(chips):
            source = lax.rem(chip + chips - t, chips) * 2 + 1 - core
            block_copy(whole, send_sem, recv_sem, source, 0).wait_recv()

    pair_copies = gather_sends(pair_in, pair_all, pair_send, pair_recv)
    for copy in pair_copies:
        copy.start()
    for copy in own_loads + loads:
        copy.wait()

    z_own = pair_all[own_block, :].astype(F32)
    hat, scale = layer_norm(z_own)
    for i, part in enumerate(gates(matmul(hat, w1[...]), c)):
        saved1[i] = part

    pair_copies += forward(pair_all, pair_send, pair_recv)
    cot_copies = gather_sends(cot_in, cot_all, cot_send, cot_recv)
    for copy in cot_copies:
        copy.start()
    wait_forwarded(pair_all, pair_send, pair_recv)

    whole_rows = tokens * tokens

    def chunks(body):
        for i in range(0, whole_rows, chunk):
            body(pl.ds(i, chunk))

    def project1(at):
        hat, _ = layer_norm(pair_all[at, :].astype(F32))
        ap, sa, bp, sb, gate = gates(matmul(hat, w1[...]), c)
        m = mask[at, :]
        a1[at, :] = rounded(m * sa * ap)
        b1[at, :] = rounded(m * sb * bp)
        gate1[at, :] = gate

    chunks(project1)
    wide = 8

    def product1(ib, carry):
        base = ib * (wide * tokens)
        sums = [jnp.zeros((tokens, c), F32) for _ in range(wide)]
        for k in range(tokens):
            block = b1[pl.ds(k, tokens, stride=tokens), :]
            for u in range(wide):
                sums[u] = sums[u] + a1[pl.ds(base + (u * tokens + k), 1), :] * block
        for u in range(wide):
            x[pl.ds(pl.multiple_of(base + u * tokens, tokens), tokens), :] = sums[u]
        return carry

    lax.fori_loop(0, tokens // wide, product1, 0)


    def finish1(at):
        y, _ = layer_norm(x[at, :])
        middle = rounded(pair_all[at, :].astype(F32) + gate1[at, :] * matmul(y, v1[...]))
        mid[at, :] = middle
        hat, _ = layer_norm(middle)
        ap, sa, bp, sb, gate = gates(matmul(hat, w2[...]), c)
        m = mask[at, :]
        a2[at, :] = rounded(m * sa * ap)
        b2[at, :] = rounded(m * sb * bp)
        gate2[at, :] = gate

    chunks(finish1)
    cot_copies += forward(cot_all, cot_send, cot_recv)
    x1_hat, x1_scale = layer_norm(x[own_block, :])
    update1 = matmul(x1_hat, v1[...])

    def product2(ib, carry):
        base = ib * wide
        sums = [jnp.zeros((tokens, c), F32) for _ in range(wide)]
        for k in range(tokens):
            block = b2[k * tokens : (k + 1) * tokens, :]
            for u in range(wide):
                sums[u] = sums[u] + a2[pl.ds(base + (k * tokens + u), 1), :] * block
        for u in range(wide):
            x[pl.ds(pl.multiple_of((base + u) * tokens, tokens), tokens), :] = sums[u]
        return carry

    lax.fori_loop(0, tokens // wide, product2, 0)

    wait_forwarded(cot_all, cot_send, cot_recv)

    def back2(at):
        hat, scale = layer_norm(x[at, :])
        dy = rounded(matmul_t(cot_all[at, :].astype(F32) * gate2[at, :], v2[...]))
        dx[at, :] = rounded(layer_norm_back(dy, hat, scale))

    chunks(back2)

    def own_rows(left, right):
        sums = [jnp.zeros((tokens, c), F32) for _ in range(rows)]
        for t in range(tokens):
            block = right(t)
            for r in range(rows):
                sums[r] = sums[r] + left(r, t) * block
        return rounded(jnp.concatenate(sums, axis=0))

    m_own = mask[own_block, :]
    cot_own = cot_all[own_block, :].astype(F32)
    mid_own = mid[own_block, :]
    y2, _ = layer_norm(x[own_block, :])
    update2 = matmul(y2, v2[...])
    gate2_own = gate2[own_block, :]
    out_ref[...] = (mid_own + gate2_own * update2).astype(BF16)
    start = me * own
    da2 = own_rows(
        lambda r, t: b2[pl.ds(start + (r * tokens + t), 1), :],
        lambda t: dx[pl.ds(t, tokens, stride=tokens), :],
    )
    db2 = own_rows(
        lambda r, t: a2[pl.ds(start + (r * tokens + t), 1), :],
        lambda t: dx[t * tokens : (t + 1) * tokens, :],
    )
    hat2, scale2 = layer_norm(mid_own)
    saved2 = gates(matmul(hat2, w2[...]), c)
    grad1 = cot_own + project_back(
        da2, db2, cot_own * update2, m_own, saved2, hat2, scale2, w2[...]
    )

    dy1 = rounded(matmul_t(grad1 * saved1[4], v1[...]))
    dx1 = rounded(layer_norm_back(dy1, x1_hat, x1_scale))
    x[0:own, :] = dx1
    for r in range(rows):
        for s in range(rows):
            send_buf[pl.ds(r * rows + s, n, stride=slotrows), :] = x[
                pl.ds(r * tokens + s, n, stride=rows), :
            ]

    def turn_block(ref, i):
        return ref.at[pl.ds(pl.multiple_of(i * slotrows, slotrows), slotrows)]

    turns = []
    for t in range(1, n):
        target = lax.rem(me + t, n)
        turns.append(
            pltpu.make_async_remote_copy(
                src_ref=turn_block(send_buf, target), dst_ref=turn_block(recv_buf, me),
                send_sem=turn_send.at[t], recv_sem=turn_recv.at[t],
                device_id=device(target), device_id_type=pl.DeviceIdType.MESH,
            )
        )
    for copy in turns:
        copy.start()
    mine = pl.ds(pl.multiple_of(me * slotrows, slotrows), slotrows)
    recv_buf[mine, :] = send_buf[mine, :]

    da1 = own_rows(
        lambda r, t: x[r * tokens + t : r * tokens + t + 1, :],
        lambda t: b1[t * tokens : (t + 1) * tokens, :],
    )
    for t in range(1, n):
        source = lax.rem(me + n - t, n)
        pltpu.make_async_remote_copy(
            src_ref=turn_block(send_buf, me), dst_ref=turn_block(recv_buf, source),
            send_sem=turn_send.at[t], recv_sem=turn_recv.at[t],
            device_id=device(source), device_id_type=pl.DeviceIdType.MESH,
        ).wait_recv()

    def turned(r, t):
        at = (t // rows) * slotrows + (t % rows) * rows + r
        return recv_buf[at : at + 1, :]

    db1 = own_rows(turned, lambda t: a1[t * tokens : (t + 1) * tokens, :])
    saved = [saved1[i] for i in range(5)]
    hat1, scale1 = layer_norm(pair_all[own_block, :].astype(F32))
    grad0 = grad1 + project_back(
        da1, db1, grad1 * update1, m_own, saved, hat1, scale1, w1[...]
    )
    grad_ref[...] = grad0.astype(BF16)
    for copy in pair_copies + cot_copies + turns:
        copy.wait_send()


def fused(n, pair, chain_counts, w1, v1, w2, v2, cotangent):
    rows, tokens, c = pair.shape
    own, whole = rows * tokens, tokens * tokens
    hbm_spec = pl.BlockSpec(memory_space=pltpu.HBM)
    vmem_spec = pl.BlockSpec(memory_space=pltpu.VMEM)
    result = jax.ShapeDtypeStruct((own, c), BF16)
    full = pltpu.VMEM((whole, c), F32)
    chunk = whole
    turn = pltpu.VMEM((n * 8, c), F32)
    both = pl.pallas_call(
        functools.partial(kernel, n, rows, tokens, chunk, tokens // chain_counts.shape[0]),
        out_shape=jax.ShapeDtypeStruct((2 * own, c), BF16),
        in_specs=[hbm_spec] * 7,
        out_specs=vmem_spec,
        scratch_shapes=[pltpu.VMEM((whole, c), BF16)] * 2
        + [pltpu.VMEM(w.shape, BF16) for w in (w1, v1, w2, v2)]
        + [pltpu.SMEM(chain_counts.shape, jnp.int32)]
        + [full] * 10
        + [pltpu.VMEM((5, own, c), F32), turn, turn]
        + [
            pltpu.SemaphoreType.DMA,
            pltpu.SemaphoreType.DMA((4,)),
            pltpu.SemaphoreType.DMA((2,)),
            pltpu.SemaphoreType.DMA((n,)),
            pltpu.SemaphoreType.DMA((n,)),
            pltpu.SemaphoreType.DMA((n,)),
            pltpu.SemaphoreType.DMA((n,)),
            pltpu.SemaphoreType.DMA((n,)),
            pltpu.SemaphoreType.DMA((n,)),
        ],
        compiler_params=pltpu.CompilerParams(
            collective_id=0, has_side_effects=True
        ),
    )(pair.reshape(own, c), chain_counts, w1, v1, w2, v2, cotangent.reshape(own, c))
    both = both.reshape((2,) + pair.shape)
    return both[0], both[1]


def solution(mesh):
    in_specs = (
        P(("grp", "row"), None, None),
        P("grp"),
        P(),
        P(),
        P(),
        P(),
        P(("grp", "row"), None, None),
    )
    out_specs = (P(("grp", "row"), None, None), P(("grp", "row"), None, None))
    n = mesh.shape["row"]

    def run(pair, chain_counts, w1, v1, w2, v2, cotangent):
        rows, tokens, c = pair.shape
        small = tokens <= 32 and rows * rows <= 8 and tokens % 8 == 0 and n % 2 == 0
        if small and (rows * tokens) % 16 == 0 and w1.shape[1] == 5 * c and c == 128:
            return fused(n, pair, chain_counts, w1, v1, w2, v2, cotangent)
        return body(pair, chain_counts, w1, v1, w2, v2, cotangent)

    return jax.shard_map(run, mesh=mesh, in_specs=in_specs, out_specs=out_specs, check_vma=False)
```

```python
import functools

import jax
import jax.numpy as jnp
from jax import lax
from jax.experimental import pallas as pl
from jax.experimental.pallas import tpu as pltpu
from jax.sharding import PartitionSpec as P


def token_valid(positions, counts, slot):
    chain = positions // slot
    labels = jnp.arange(counts.shape[0], dtype=jnp.int32)
    own = jnp.sum(jnp.where(chain[:, None] == labels[None, :], counts[None, :], 0), axis=1)
    return (positions % slot < own).astype(jnp.float32)


def normalize(values):
    center = values - jnp.mean(values, axis=-1, keepdims=True)
    spread = jnp.mean(center * center, axis=-1, keepdims=True)
    return center * jax.lax.rsqrt(spread + 1e-05)


def project(zfloat, mask, weight):
    hidden = weight.shape[1] // 4 - weight.shape[0] // 4
    width = zfloat.shape[-1]
    normed = normalize(zfloat).astype(jnp.bfloat16)
    lead = normed.shape[:-1]
    mixed = jnp.dot(normed.reshape(-1, width), weight, preferred_element_type=jnp.float32)
    mixed = mixed.reshape(lead + (weight.shape[1],))
    a_proj = mixed[..., :hidden]
    a_gate = mixed[..., hidden : 2 * hidden]
    b_proj = mixed[..., 2 * hidden : 3 * hidden]
    b_gate = mixed[..., 3 * hidden : 4 * hidden]
    out_gate = jax.nn.sigmoid(mixed[..., 4 * hidden :])
    left = (mask[..., None] * jax.nn.sigmoid(a_gate) * a_proj).astype(jnp.bfloat16)
    right = (mask[..., None] * jax.nn.sigmoid(b_gate) * b_proj).astype(jnp.bfloat16)
    return (left, right, out_gate)


def finish(contracted, out_gate, zfloat, final):
    normed = normalize(contracted).astype(jnp.bfloat16)
    lead = normed.shape[:-1]
    update = jnp.dot(normed.reshape(-1, final.shape[0]), final, preferred_element_type=jnp.float32)
    return zfloat + out_gate * update.reshape(lead + (final.shape[1],))


def contract(form, first, second):
    return jnp.einsum(form, first, second, preferred_element_type=jnp.float32)


def body(pair, chain_counts, w_out_proj, w_out_final, w_in_proj, w_in_final, cotangent):
    rows = pair.shape[0]
    tokens = pair.shape[1]
    slot = tokens // chain_counts.shape[0]
    positions = jnp.arange(tokens, dtype=jnp.int32)
    own_rows = lax.axis_index("row") * rows + jnp.arange(rows, dtype=jnp.int32)
    mask = (
        token_valid(own_rows, chain_counts, slot)[:, None]
        * token_valid(positions, chain_counts, slot)[None, :]
    )
    start_float = pair.astype(jnp.float32)
    left1, right1, gate1 = project(start_float, mask, w_out_proj)
    inner1 = contract("ikc,jkc->ijc", left1, lax.all_gather(right1, "row", axis=0, tiled=True))
    middle = finish(inner1, gate1, start_float, w_out_final).astype(jnp.bfloat16)
    middle_float = middle.astype(jnp.float32)
    left2, right2, gate2 = project(middle_float, mask, w_in_proj)
    left_turned, right_turned = (
        lax.all_to_all(left2, "row", split_axis=1, concat_axis=0, tiled=True),
        lax.all_to_all(right2, "row", split_axis=1, concat_axis=0, tiled=True),
    )
    inner2 = contract(
        "kic,kjc->ijc", left_turned, lax.all_gather(right_turned, "row", axis=1, tiled=True)
    )
    pair_out = finish(inner2, gate2, middle_float, w_in_final).astype(jnp.bfloat16)
    _, finish_back2 = jax.vjp(
        lambda x, g, z: finish(x, g, z, w_in_final), inner2, gate2, middle_float
    )
    d_inner2, d_gate2, d_direct1 = finish_back2(cotangent.astype(jnp.float32))
    d_inner2 = d_inner2.astype(jnp.bfloat16)
    piece = lax.all_gather(d_inner2, "row", axis=0, tiled=True)
    block = contract("kjc,ijc->kic", right2, piece)
    d_right = contract("kic,ijc->kjc", left2, piece)
    _, project_back2 = jax.vjp(lambda z: project(z, mask, w_in_proj), middle_float)
    (d_proj1,) = project_back2((block.astype(jnp.bfloat16), d_right.astype(jnp.bfloat16), d_gate2))
    grad_middle = d_direct1 + d_proj1
    _, finish_back1 = jax.vjp(
        lambda x, g, z: finish(x, g, z, w_out_final), inner1, gate1, start_float
    )
    d_inner1, d_gate1, d_direct0 = finish_back1(grad_middle)
    d_inner1 = d_inner1.astype(jnp.bfloat16)
    d_left1 = contract("ijc,jkc->ikc", d_inner1, lax.all_gather(right1, "row", axis=0, tiled=True))
    d_turned = lax.all_to_all(d_inner1, "row", split_axis=1, concat_axis=0, tiled=True)
    d_right1 = contract("ijc,ikc->jkc", d_turned, lax.all_gather(left1, "row", axis=0, tiled=True))
    _, project_back1 = jax.vjp(lambda z: project(z, mask, w_out_proj), start_float)
    (d_proj0,) = project_back1(
        (d_left1.astype(jnp.bfloat16), d_right1.astype(jnp.bfloat16), d_gate1)
    )
    pair_grad = (d_direct0 + d_proj0).astype(jnp.bfloat16)
    return (pair_out, pair_grad)


F32 = jnp.float32
BF16 = jnp.bfloat16
EPS = 1e-05


def sigmoid(x):
    return 0.5 * jnp.tanh(0.5 * x) + 0.5


def matmul(x, w):
    return jnp.dot(x.astype(BF16), w, preferred_element_type=F32)


def matmul_t(x, w):
    return lax.dot_general(x.astype(BF16), w, (((1,), (1,)), ((), ())), preferred_element_type=F32)


def mean(x):
    return jnp.mean(x, axis=-1, keepdims=True)


def mean_by_matmul(x):
    c = x.shape[1]
    return jnp.dot(x.astype(BF16), jnp.full((c, c), 1.0 / c, BF16), preferred_element_type=F32)


def layer_norm(x):
    center = x - mean(x)
    scale = lax.rsqrt(mean_by_matmul(center * center) + EPS)
    return center * scale, scale


def layer_norm_back(grad, hat, scale):
    return scale * (grad - mean(grad) - hat * mean(grad * hat))


def rounded(x):
    return x.astype(BF16).astype(F32)


def gates(hidden, c):
    part = [hidden[:, i * c : (i + 1) * c] for i in range(5)]
    return part[0], sigmoid(part[1]), part[2], sigmoid(part[3]), sigmoid(part[4])


def project_back(da, db, dgate, mask, saved, hat, scale, weight):
    ap, sa, bp, sb, gate = saved
    ma, mb = mask * da * sa, mask * db * sb
    parts = [ma, ma * ap * (1.0 - sa), mb, mb * bp * (1.0 - sb), dgate * gate * (1.0 - gate)]
    dhidden = jnp.concatenate([p.astype(BF16) for p in parts], axis=1)
    return layer_norm_back(rounded(matmul_t(dhidden, weight)), hat, scale)


def kernel(
    n, rows, tokens, chunk, slot,
    pair_in, counts_in, w1_in, v1_in, w2_in, v2_in, cot_in,
    both_ref,
    pair_all, cot_all, w1, v1, w2, v2,
    counts, mask, a1, b1, gate1, x, mid, a2, b2, gate2, dx, saved1, send_buf, recv_buf,
    counts_sem, local_sem, own_sem, pair_send, pair_recv, cot_send, cot_recv, turn_send, turn_recv,
):
    me = lax.axis_index("row")
    core = lax.rem(me, 2)
    chip = me // 2
    chips = n // 2
    sibling = me + 1 - 2 * core
    own = rows * tokens
    c = both_ref.shape[1]
    out_ref = both_ref.at[0:own]
    grad_ref = both_ref.at[own : 2 * own]
    slotrows = 8

    def device(i):
        return {"row": i}

    loads = [
        pltpu.make_async_copy(s, d, local_sem.at[i])
        for i, (s, d) in enumerate([(w1_in, w1), (v1_in, v1), (w2_in, w2), (v2_in, v2)])
    ]
    own_block = pl.ds(pl.multiple_of(me * own, own), own)
    own_loads = [
        pltpu.make_async_copy(pair_in, pair_all.at[own_block], own_sem.at[0]),
        pltpu.make_async_copy(cot_in, cot_all.at[own_block], own_sem.at[1]),
    ]
    count_load = pltpu.make_async_copy(counts_in, counts, counts_sem)
    for copy in [count_load] + own_loads + loads:
        copy.start()

    barrier = pltpu.get_barrier_semaphore()
    for t in range(1, n):
        pl.semaphore_signal(
            barrier, inc=1, device_id=device(lax.rem(me + t, n)),
            device_id_type=pl.DeviceIdType.MESH,
        )

    def valid(index):
        chain = index // slot
        count = jnp.zeros(index.shape, jnp.int32)
        for i in range(counts.shape[0]):
            count = jnp.where(chain == i, counts[i], count)
        return jnp.where(index - chain * slot < count, 1.0, 0.0)

    count_load.wait()
    second = valid(lax.broadcasted_iota(jnp.int32, (tokens, c), 0))
    for i in range(tokens):
        first = valid(jnp.full((tokens, c), i, jnp.int32))
        mask[i * tokens : (i + 1) * tokens, :] = first * second

    pl.semaphore_wait(barrier, n - 1)

    def gather_sends(source, whole, send_sem, recv_sem):
        copies = []
        for t in range(chips):
            target = sibling if t == 0 else lax.rem(chip + t, chips) * 2 + core
            copies.append(
                pltpu.make_async_remote_copy(
                    src_ref=source, dst_ref=whole.at[own_block],
                    send_sem=send_sem.at[t], recv_sem=recv_sem.at[me],
                    device_id=device(target), device_id_type=pl.DeviceIdType.MESH,
                )
            )
        return copies

    def block_copy(whole, send_sem, recv_sem, index, send_index):
        block = whole.at[pl.ds(pl.multiple_of(index * own, own), own)]
        return pltpu.make_async_remote_copy(
            src_ref=block, dst_ref=block,
            send_sem=send_sem.at[send_index], recv_sem=recv_sem.at[index],
            device_id=device(sibling), device_id_type=pl.DeviceIdType.MESH,
        )

    def forward(whole, send_sem, recv_sem):
        copies = []
        for t in range(1, chips):
            source = lax.rem(chip + chips - t, chips) * 2 + core
            copy = block_copy(whole, send_sem, recv_sem, source, chips - 1 + t)
            copy.wait_recv()
            copy.start()
            copies.append(copy)
        return copies

    def wait_forwarded(whole, send_sem, recv_sem):
        for t in range(chips):
            source = lax.rem(chip + chips - t, chips) * 2 + 1 - core
            block_copy(whole, send_sem, recv_sem, source, 0).wait_recv()

    pair_copies = gather_sends(pair_in, pair_all, pair_send, pair_recv)
    for copy in pair_copies:
        copy.start()
    for copy in own_loads + loads:
        copy.wait()

    z_own = pair_all[own_block, :].astype(F32)
    hat, scale = layer_norm(z_own)
    for i, part in enumerate(gates(matmul(hat, w1[...]), c)):
        saved1[i] = part

    pair_copies += forward(pair_all, pair_send, pair_recv)
    cot_copies = gather_sends(cot_in, cot_all, cot_send, cot_recv)
    for copy in cot_copies:
        copy.start()
    wait_forwarded(pair_all, pair_send, pair_recv)

    whole_rows = tokens * tokens

    def chunks(body):
        for i in range(0, whole_rows, chunk):
            body(pl.ds(i, chunk))

    def project1(at):
        hat, _ = layer_norm(pair_all[at, :].astype(F32))
        ap, sa, bp, sb, gate = gates(matmul(hat, w1[...]), c)
        m = mask[at, :]
        a1[at, :] = rounded(m * sa * ap)
        b1[at, :] = rounded(m * sb * bp)
        gate1[at, :] = gate

    chunks(project1)
    wide = 8

    def product1(ib, carry):
        base = ib * (wide * tokens)
        sums = [jnp.zeros((tokens, c), F32) for _ in range(wide)]
        for k in range(tokens):
            block = b1[pl.ds(k, tokens, stride=tokens), :]
            for u in range(wide):
                sums[u] = sums[u] + a1[pl.ds(base + (u * tokens + k), 1), :] * block
        for u in range(wide):
            x[pl.ds(base + u * tokens, tokens), :] = sums[u]
        return carry

    for ib in range(tokens // wide):
        product1(ib, 0)


    def finish1(at):
        y, _ = layer_norm(x[at, :])
        middle = rounded(pair_all[at, :].astype(F32) + gate1[at, :] * matmul(y, v1[...]))
        mid[at, :] = middle
        hat, _ = layer_norm(middle)
        ap, sa, bp, sb, gate = gates(matmul(hat, w2[...]), c)
        m = mask[at, :]
        a2[at, :] = rounded(m * sa * ap)
        b2[at, :] = rounded(m * sb * bp)
        gate2[at, :] = gate

    chunks(finish1)
    cot_copies += forward(cot_all, cot_send, cot_recv)
    x1_hat, x1_scale = layer_norm(x[own_block, :])
    update1 = matmul(x1_hat, v1[...])

    def product2(ib, carry):
        base = ib * wide
        sums = [jnp.zeros((tokens, c), F32) for _ in range(wide)]
        for k in range(tokens):
            block = b2[k * tokens : (k + 1) * tokens, :]
            for u in range(wide):
                sums[u] = sums[u] + a2[pl.ds(base + (k * tokens + u), 1), :] * block
        for u in range(wide):
            x[pl.ds((base + u) * tokens, tokens), :] = sums[u]
        return carry

    for ib in range(tokens // wide):
        product2(ib, 0)

    wait_forwarded(cot_all, cot_send, cot_recv)

    def back2(at):
        hat, scale = layer_norm(x[at, :])
        dy = rounded(matmul_t(cot_all[at, :].astype(F32) * gate2[at, :], v2[...]))
        dx[at, :] = rounded(layer_norm_back(dy, hat, scale))

    chunks(back2)

    def own_rows(left, right):
        sums = [jnp.zeros((tokens, c), F32) for _ in range(rows)]
        for t in range(tokens):
            block = right(t)
            for r in range(rows):
                sums[r] = sums[r] + left(r, t) * block
        return rounded(jnp.concatenate(sums, axis=0))

    m_own = mask[own_block, :]
    cot_own = cot_all[own_block, :].astype(F32)
    mid_own = mid[own_block, :]
    y2, _ = layer_norm(x[own_block, :])
    update2 = matmul(y2, v2[...])
    gate2_own = gate2[own_block, :]
    out_ref[...] = (mid_own + gate2_own * update2).astype(BF16)
    start = me * own
    da2 = own_rows(
        lambda r, t: b2[pl.ds(start + (r * tokens + t), 1), :],
        lambda t: dx[pl.ds(t, tokens, stride=tokens), :],
    )
    db2 = own_rows(
        lambda r, t: a2[pl.ds(start + (r * tokens + t), 1), :],
        lambda t: dx[t * tokens : (t + 1) * tokens, :],
    )
    hat2, scale2 = layer_norm(mid_own)
    saved2 = gates(matmul(hat2, w2[...]), c)
    grad1 = cot_own + project_back(
        da2, db2, cot_own * update2, m_own, saved2, hat2, scale2, w2[...]
    )

    dy1 = rounded(matmul_t(grad1 * saved1[4], v1[...]))
    dx1 = rounded(layer_norm_back(dy1, x1_hat, x1_scale))
    x[0:own, :] = dx1
    for r in range(rows):
        for s in range(rows):
            send_buf[pl.ds(r * rows + s, n, stride=slotrows), :] = x[
                pl.ds(r * tokens + s, n, stride=rows), :
            ]

    def turn_block(ref, i):
        return ref.at[pl.ds(pl.multiple_of(i * slotrows, slotrows), slotrows)]

    turns = []
    for t in range(1, n):
        target = lax.rem(me + t, n)
        turns.append(
            pltpu.make_async_remote_copy(
                src_ref=turn_block(send_buf, target), dst_ref=turn_block(recv_buf, me),
                send_sem=turn_send.at[t], recv_sem=turn_recv.at[t],
                device_id=device(target), device_id_type=pl.DeviceIdType.MESH,
            )
        )
    for copy in turns:
        copy.start()
    mine = pl.ds(pl.multiple_of(me * slotrows, slotrows), slotrows)
    recv_buf[mine, :] = send_buf[mine, :]

    da1 = own_rows(
        lambda r, t: x[r * tokens + t : r * tokens + t + 1, :],
        lambda t: b1[t * tokens : (t + 1) * tokens, :],
    )
    for t in range(1, n):
        source = lax.rem(me + n - t, n)
        pltpu.make_async_remote_copy(
            src_ref=turn_block(send_buf, me), dst_ref=turn_block(recv_buf, source),
            send_sem=turn_send.at[t], recv_sem=turn_recv.at[t],
            device_id=device(source), device_id_type=pl.DeviceIdType.MESH,
        ).wait_recv()

    def turned(r, t):
        at = (t // rows) * slotrows + (t % rows) * rows + r
        return recv_buf[at : at + 1, :]

    db1 = own_rows(turned, lambda t: a1[t * tokens : (t + 1) * tokens, :])
    saved = [saved1[i] for i in range(5)]
    hat1, scale1 = layer_norm(pair_all[own_block, :].astype(F32))
    grad0 = grad1 + project_back(
        da1, db1, grad1 * update1, m_own, saved, hat1, scale1, w1[...]
    )
    grad_ref[...] = grad0.astype(BF16)
    for copy in pair_copies + cot_copies + turns:
        copy.wait_send()


def fused(n, pair, chain_counts, w1, v1, w2, v2, cotangent):
    rows, tokens, c = pair.shape
    own, whole = rows * tokens, tokens * tokens
    hbm_spec = pl.BlockSpec(memory_space=pltpu.HBM)
    vmem_spec = pl.BlockSpec(memory_space=pltpu.VMEM)
    result = jax.ShapeDtypeStruct((own, c), BF16)
    full = pltpu.VMEM((whole, c), F32)
    chunk = whole
    turn = pltpu.VMEM((n * 8, c), F32)
    both = pl.pallas_call(
        functools.partial(kernel, n, rows, tokens, chunk, tokens // chain_counts.shape[0]),
        out_shape=jax.ShapeDtypeStruct((2 * own, c), BF16),
        in_specs=[hbm_spec] * 7,
        out_specs=vmem_spec,
        scratch_shapes=[pltpu.VMEM((whole, c), BF16)] * 2
        + [pltpu.VMEM(w.shape, BF16) for w in (w1, v1, w2, v2)]
        + [pltpu.SMEM(chain_counts.shape, jnp.int32)]
        + [full] * 10
        + [pltpu.VMEM((5, own, c), F32), turn, turn]
        + [
            pltpu.SemaphoreType.DMA,
            pltpu.SemaphoreType.DMA((4,)),
            pltpu.SemaphoreType.DMA((2,)),
            pltpu.SemaphoreType.DMA((n,)),
            pltpu.SemaphoreType.DMA((n,)),
            pltpu.SemaphoreType.DMA((n,)),
            pltpu.SemaphoreType.DMA((n,)),
            pltpu.SemaphoreType.DMA((n,)),
            pltpu.SemaphoreType.DMA((n,)),
        ],
        compiler_params=pltpu.CompilerParams(
            collective_id=0, has_side_effects=True
        ),
    )(pair.reshape(own, c), chain_counts, w1, v1, w2, v2, cotangent.reshape(own, c))
    both = both.reshape((2,) + pair.shape)
    return both[0], both[1]


def solution(mesh):
    in_specs = (
        P(("grp", "row"), None, None),
        P("grp"),
        P(),
        P(),
        P(),
        P(),
        P(("grp", "row"), None, None),
    )
    out_specs = (P(("grp", "row"), None, None), P(("grp", "row"), None, None))
    n = mesh.shape["row"]

    def run(pair, chain_counts, w1, v1, w2, v2, cotangent):
        rows, tokens, c = pair.shape
        small = tokens <= 32 and rows * rows <= 8 and tokens % 8 == 0 and n % 2 == 0
        if small and (rows * tokens) % 16 == 0 and w1.shape[1] == 5 * c and c == 128:
            return fused(n, pair, chain_counts, w1, v1, w2, v2, cotangent)
        return body(pair, chain_counts, w1, v1, w2, v2, cotangent)

    return jax.shard_map(run, mesh=mesh, in_specs=in_specs, out_specs=out_specs, check_vma=False)
```
